128 devices in a mesh: freq: 4 (over y), blk: 32 (over x, z, core).
Axes of the slice: x: 4, y: 4, z: 4, core: 2. Of those that a mesh axis runs over, the one named last changes fastest.
Arguments:
- voltages: float32 [32, 32, 2, 128, 256], P('blk', None, None, 'freq'), may hold values from -6 to 6
- pair_table: int32 [544, 2], P('blk'), may hold values from 0 to 31, as said below
- bad_feeds: int32 [64], replicated, may hold values from 0 to 2047
Outputs:
- visibilities: float32 [544, 32, 2, 128, 128], P('blk', 'freq')
The draws below stay inside these ranges and needn't reach their ends.
Inputs may be any that keep to these rules, and one draw needn't show every extreme that they name: `pair_table`: device k of blk holds blocks k * 1 to k + 1 - 1 and tiles k * 17 to k * 17 + 16. Of its tiles, the first 1 (2) / 2 name two of its own blocks; then for d = 1 to 15 in turn, 1 tiles each name one own block and one block of device k + d; the last (2) / 2 name one own block and one block of device k + 16; device numbers are taken modulo 32, and either block of a tile may come first. Every unordered pair of blocks is named at least once.
All inputs are finite; a program needn't handle non-finite values.
Results may differ from the reference program's by a relative error of at most 0.000098.
Values sent between devices are 32-bit elements; how exact they have to be, the bound alone decides.
No kernel may reach another device: no remote copies, remote signals or barrier semaphores. Data moves between devices by JAX's collectives and lax.ppermute only.
A program may use at most 128 MiB of HBM per device.

```python
import jax
import jax.numpy as jnp
from jax import lax

BI = 128
SAMP = 256
NBAD = 64
NB = 32
FEEDS = 2048
CHAN = 32
BPD = 1


def draw_pair_table(key, part):
    key = jax.random.fold_in(key, 5)
    devices = NB // BPD
    half = devices // 2
    square = BPD * BPD
    shared = (square + 1) // 2
    order_key, flip_key, turn_key, group_key = jax.random.split(key, 4)
    order = jax.random.permutation(order_key, square).astype(jnp.int32)
    flips = jax.random.randint(flip_key, (devices,), 0, 2)
    lefts = []
    rights = []
    for device in range(devices):
        base = device * BPD
        for one in range(BPD):
            for two in range(one, BPD):
                lefts.append(jnp.array([base + one], jnp.int32))
                rights.append(jnp.array([base + two], jnp.int32))
        for step in range(1, half):
            other = (device + step) % devices * BPD
            mixed = jax.random.permutation(jax.random.fold_in(group_key, device * devices + step), square).astype(jnp.int32)
            lefts.append(base + mixed // BPD)
            rights.append(other + mixed % BPD)
        lower = device % half
        upper = lower + half
        count_low = jnp.where(flips[lower] == 1, shared, square - shared)
        slot = jnp.arange(shared, dtype=jnp.int32)
        if device < half:
            pick = slot
        else:
            pick = count_low + slot
            pick = jnp.where(pick < square, pick, slot)
        tile = order[pick]
        low_block = (lower * BPD + tile // BPD).astype(jnp.int32)
        up_block = (upper * BPD + tile % BPD).astype(jnp.int32)
        if device < half:
            lefts.append(low_block)
            rights.append(up_block)
        else:
            lefts.append(up_block)
            rights.append(low_block)
    left = jnp.concatenate(lefts)
    right = jnp.concatenate(rights)
    turned = jax.random.randint(turn_key, left.shape, 0, 2) == 1
    return jnp.stack([jnp.where(turned, right, left), jnp.where(turned, left, right)], axis=1).astype(jnp.int32)


def place_ends(values, key, least, top_value):
    longest = values.shape.index(max(values.shape))
    spots = []
    for shift in (0, 1):
        where = [jax.random.randint(jax.random.fold_in(key, axis), (), 0, length) for axis, length in enumerate(values.shape)]
        where[longest] = (where[longest] + shift) % values.shape[longest]
        spots.append(tuple(where))
    return values.at[spots[0]].set(least).at[spots[1]].set(top_value)


def levels(key, dims, shards, least, top_value):
    gain = 1.0
    for dim, blocks in shards:
        draws = jax.random.uniform(jax.random.fold_in(jax.random.fold_in(key, 6), dim), (blocks,), jnp.float32, least / len(shards), top_value / len(shards))
        gain = gain * jnp.repeat(jnp.exp(draws), dims[dim] // blocks).reshape((-1,) + (1,) * (len(dims) - 1 - dim))
    return gain


def noise(stream_key, dims, deviation, bound, shards=(), kind=jnp.bfloat16):
    loudness = levels(stream_key, dims, shards, -0.22, 0.18) if shards else 1.0
    values = jax.random.normal(stream_key, dims, jnp.float32) * deviation * loudness
    return jnp.minimum(jnp.maximum(values, -bound), bound).astype(kind)


def setup_inputs(seed: int = 0) -> dict:
    keys = jax.random.split(jax.random.key(seed), 4)
    return {
        "voltages": noise(keys[0], (NB, CHAN, 2, BI, SAMP), 1.0, 6.0, ((0, 32), (3, 4)), jnp.float32),
        "pair_table": draw_pair_table(jax.random.fold_in(keys[3], 71), 0),
        "bad_feeds": place_ends(jax.random.randint(keys[2], (NBAD,), 0, FEEDS), jax.random.fold_in(keys[2], 1), 0, FEEDS - 1).astype(jnp.int32),
    }


def reference(voltages, pair_table, bad_feeds):
    inputs = jnp.arange(NB * BI, dtype=jnp.int32).reshape(NB, BI)
    flagged = jnp.any((inputs // 2)[:, :, None] == bad_feeds[None, None, :], axis=-1)
    keep = jnp.where(flagged, 0.0, 1.0).astype(jnp.float32)
    clean = voltages * keep[:, None, None, :, None]
    scale = 1.0 / SAMP

    def one_tile(pair):
        left = clean[pair[0]]
        right = clean[pair[1]]
        prec = lax.Precision.HIGHEST
        real = jnp.einsum("cps,cqs->cpq", left[:, 0], right[:, 0], precision=prec) + jnp.einsum("cps,cqs->cpq", left[:, 1], right[:, 1], precision=prec)
        imag = jnp.einsum("cps,cqs->cpq", left[:, 1], right[:, 0], precision=prec) - jnp.einsum("cps,cqs->cpq", left[:, 0], right[:, 1], precision=prec)
        return jnp.stack([real, imag], axis=1) * scale

    return lax.map(one_tile, pair_table)
```

```python
import functools

import jax
import jax.numpy as jnp
from jax import lax
from jax.experimental import pallas as pl
from jax.experimental.pallas import tpu as pltpu
from jax.sharding import PartitionSpec as P

CHUNKS = (2, 2, 2, 2)
SIDE = 4


def place(x, z, core):
    return ((x % SIDE) * SIDE + z % SIDE) * 2 + core


def fetch(value, source_of):
    pairs = []
    for x in range(SIDE):
        for z in range(SIDE):
            for core in range(2):
                source = source_of(x, z, core)
                if source is not None:
                    pairs.append((place(*source), place(x, z, core)))
    return lax.ppermute(value, "blk", pairs)


def side(core, flip):
    return 1 if (core == 0) != flip else -1


def split(value):
    high = value.astype(jnp.bfloat16)
    low = (value - high.astype(jnp.float32)).astype(jnp.bfloat16)
    return high, low


def tiles_kernel(count, first, table, own_ref, *refs):
    far_refs = refs[:count]
    out_ref, held, sems = refs[-3:]
    step = pl.program_id(0)
    steps = pl.num_programs(0)
    slot = lax.rem(step, 2)

    def copy(index, which):
        return pltpu.make_async_copy(
            held.at[which, index], out_ref.at[table[0, index], first + step], sems.at[which, index]
        )

    @pl.when(step >= 2)
    def _():
        for index in range(count):
            copy(index, slot).wait()

    own = [split(own_ref[0, part]) for part in range(2)]
    for index in range(count):
        far = [split(far_refs[index][0, part]) for part in range(2)]
        swapped = table[1, index] != 0
        left = [[jnp.where(swapped, f, o) for f, o in zip(a, b)] for a, b in zip(far, own)]
        right = [[jnp.where(swapped, o, f) for f, o in zip(a, b)] for a, b in zip(far, own)]
        rows_high = jnp.concatenate([left[0][0], left[1][0]], axis=1)
        rows_low = jnp.concatenate([left[0][1], left[1][1]], axis=1)
        columns = []
        for level in range(2):
            real = jnp.concatenate([right[0][level], right[1][level]], axis=1)
            imag = jnp.concatenate([-right[1][level], right[0][level]], axis=1)
            columns.append(jnp.concatenate([real, imag], axis=0))
        dims = (((1,), (1,)), ((), ()))
        both = lax.dot_general(
            jnp.concatenate([rows_high, rows_low], axis=0), columns[0], dims, preferred_element_type=jnp.float32
        )
        cross = lax.dot_general(rows_high, columns[1], dims, preferred_element_type=jnp.float32)
        width = own_ref.shape[2]
        total = (both[:width] + (both[width:] + cross)) * (1.0 / own_ref.shape[3])
        held[slot, index, 0] = total[:, :width]
        held[slot, index, 1] = total[:, width:]
        copy(index, slot).start()

    @pl.when(step == steps - 1)
    def _():
        for index in range(count):
            copy(index, slot).wait()

        @pl.when(steps > 1)
        def _():
            for index in range(count):
                copy(index, 1 - slot).wait()


def correlate(visibility, shape, own, fars, table, first):
    count = len(fars)
    channels, parts, width, samples = own.shape
    block = pl.BlockSpec((1, parts, width, samples), lambda step, table: (step, 0, 0, 0))
    anywhere = pl.BlockSpec(memory_space=pl.ANY)
    before = [] if visibility is None else [visibility]
    return pl.pallas_call(
        functools.partial(tiles_kernel, count, first),
        grid_spec=pltpu.PrefetchScalarGridSpec(
            num_scalar_prefetch=1,
            grid=(channels,),
            in_specs=[block] * (count + 1) + [anywhere] * len(before),
            out_specs=anywhere,
            scratch_shapes=[
                pltpu.VMEM((2, count, 2, width, width), jnp.float32),
                pltpu.SemaphoreType.DMA((2, count)),
            ],
        ),
        out_shape=jax.ShapeDtypeStruct(shape, jnp.float32),
        input_output_aliases={count + 2: 0} if before else {},
        compiler_params=pltpu.CompilerParams(vmem_limit_bytes=24 * 1024 * 1024),
        cost_estimate=pl.CostEstimate(
            flops=channels * count * 2 * 3 * width * 2 * width * samples * 2,
            bytes_accessed=4 * channels * parts * width * ((count + 1) * samples + count * width),
            transcendentals=0,
        ),
        name="tiles",
    )(table, own, *fars, *before)


def shards(voltages, pair_table, bad_feeds):
    here = lax.axis_index("blk").astype(jnp.int32)
    freq = lax.axis_index("freq").astype(jnp.int32)
    freq_count = lax.axis_size("freq")
    blk_count = lax.axis_size("blk")
    _, channels, parts, rows, samples = voltages.shape
    group = channels // freq_count
    width = rows * freq_count
    z = (here // 2) % SIDE
    core = here % 2

    inputs = here * width + freq * rows + jnp.arange(rows, dtype=jnp.int32)
    flagged = jnp.any((inputs // 2)[:, None] == bad_feeds[None, :], axis=-1)
    keep = jnp.where(flagged, 0.0, 1.0).astype(jnp.float32)[:, None]

    swaps = (pair_table[:, 0] != here).astype(jnp.int32)

    def table_of(steps):
        wanted = jnp.stack(steps).astype(jnp.int32)
        return jnp.stack([wanted, jnp.take(swaps, wanted)])

    near = jnp.where(core == 0, 1, 3)
    far_side = jnp.where(core == 0, 3, 1)

    def row_ahead(distance):
        return jnp.where(z + distance >= SIDE, distance, distance + SIDE)

    def row_own(distance):
        return jnp.where(z + distance >= SIDE, distance + SIDE, distance)

    def pair_of(of_mine, of_other):
        return [2 * of_mine, jnp.where(core == 0, 2 * of_other + 1, 2 * of_other - 1)]

    four = jnp.int32(SIDE)
    two = jnp.int32(2)
    slots = {
        "q0": pair_of(four, four),
        "qa": pair_of(row_ahead(near), row_ahead(far_side)),
        "qb": pair_of(row_ahead(far_side), row_ahead(near)),
        "q2": pair_of(row_ahead(two), row_ahead(two)),
        "sa": pair_of(row_own(near), row_own(far_side)),
        "sb": pair_of(row_own(far_side), row_own(near)),
        "x2": pair_of(row_own(two), row_own(two)),
        "rc": [jnp.int32(16), jnp.where(core == 0, 1, 15), jnp.int32(0)],
    }
    tables = {name: table_of(steps) for name, steps in slots.items()}

    def corner_turn(first, count):
        def piece(shift):
            start = ((freq + shift) % freq_count) * group + first
            return lax.dynamic_slice_in_dim(voltages[0], start, count, 0) * keep

        pieces = [piece(0)]
        for shift in (1, 2, 3):
            pairs = [(source, (source + shift) % freq_count) for source in range(freq_count)]
            pieces.append(lax.ppermute(piece(shift), "freq", pairs))
        parts_by_source = []
        for source in range(freq_count):
            shift = (freq - source) % freq_count
            parts_by_source.append(lax.select_n(shift, *pieces))
        return jnp.concatenate(parts_by_source, axis=2)

    visibility = None
    shape = (pair_table.shape[0], group, parts, width, width)

    first = 0
    for number, count in enumerate(CHUNKS):
        def scoped(name, value, source_of):
            with jax.named_scope(f"{name}_{number}"):
                return fetch(value, source_of)

        def exchanged(name, value):
            return scoped(name + "_core", value, lambda x, z, c: (x, z, 1 - c))

        with jax.named_scope(f"turn_{number}"):
            own = corner_turn(first, count)
        q0 = scoped("q0", own, lambda x, z, c: (x + 1, z, c))
        w = scoped("w", own, lambda x, z, c: (x - 1, z, c) if z >= 2 else None)
        qa = scoped("qa", q0, lambda x, z, c: (x, z + side(c, False), c))
        qb = scoped("qb", q0, lambda x, z, c: (x, z + side(c, True), c))
        rc = scoped(
            "rc", jnp.where(z >= 2, w, q0), lambda x, z, c: (x - 1, z, c) if z >= 2 else (x + 1, z, c)
        )
        q2 = scoped("q2", qa, lambda x, z, c: (x, z + side(c, False), c))
        down = z >= 1
        up = z == SIDE - 1
        sa = scoped(
            "sa", jnp.where(jnp.where(core == 0, down, up), own, rc), lambda x, z, c: (x, z + side(c, False), c)
        )
        sb = scoped(
            "sb", jnp.where(jnp.where(core == 0, up, down), own, rc), lambda x, z, c: (x, z + side(c, True), c)
        )
        x2 = scoped("x2", q2, lambda x, z, c: (x - 1, z, c) if z <= 1 else (x + 1, z, c))

        for name, value in (("q0", q0), ("qa", qa), ("qb", qb)):
            visibility = correlate(visibility, shape, own, [value, exchanged(name, value)], tables[name], first)
        mixed = exchanged("rc", jnp.where(core == 0, rc, own))
        visibility = correlate(visibility, shape, own, [rc, mixed, own], tables["rc"], first)
        for name, value in (("q2", q2), ("sa", sa), ("sb", sb), ("x2", x2)):
            visibility = correlate(visibility, shape, own, [value, exchanged(name, value)], tables[name], first)
        first += count
    return visibility


def solution(mesh):
    placed = (P("blk", None, None, "freq", None), P("blk", None), P())
    return jax.shard_map(
        shards,
        mesh=mesh,
        in_specs=placed,
        out_specs=P("blk", "freq", None, None, None),
        check_vma=False,
    )
```

```python
import functools

import jax
import jax.numpy as jnp
from jax import lax
from jax.experimental import pallas as pl
from jax.experimental.pallas import tpu as pltpu
from jax.sharding import PartitionSpec as P

CHUNKS = (4, 4)
SIDE = 4


def place(x, z, core):
    return ((x % SIDE) * SIDE + z % SIDE) * 2 + core


def fetch(value, source_of):
    pairs = []
    for x in range(SIDE):
        for z in range(SIDE):
            for core in range(2):
                source = source_of(x, z, core)
                if source is not None:
                    pairs.append((place(*source), place(x, z, core)))
    return lax.ppermute(value, "blk", pairs)


def side(core, flip):
    return 1 if (core == 0) != flip else -1


def after(value, *others):
    return lax.optimization_barrier((value, *others))[0]


def position(info):
    here = info[0]
    return lax.rem(lax.div(here, 2), SIDE), lax.rem(here, 2)


def tile_of(slot, info):
    kind, distance_0, distance_1, exchanged = slot
    z, core = position(info)
    if kind == "own":
        return jnp.int32(0)
    if kind == "mixed":
        return jnp.where(core == 0, 1, 15)
    mine = jnp.where(core == 0, distance_0, distance_1)
    other = jnp.where(core == 0, distance_1, distance_0)
    distance = other if exchanged else mine
    wraps = z + distance >= SIDE
    if kind == "ahead":
        chips = jnp.where(wraps, distance, distance + SIDE)
    else:
        chips = jnp.where(wraps, distance + SIDE, distance)
    if kind == "two":
        chips = jnp.int32(2 * SIDE)
    if exchanged:
        return jnp.where(core == 0, 2 * chips + 1, 2 * chips - 1)
    return 2 * chips


def split(value):
    high = value.astype(jnp.bfloat16)
    low = (value - high.astype(jnp.float32)).astype(jnp.bfloat16)
    return high, low


def tiles_kernel(slots, first, info, own_ref, *refs):
    count = len(slots)
    far_refs = refs[: count - sum(slot[0] == "own" for slot in slots)]
    out_ref, held, sems = refs[-3:]
    channels, _, width, samples = own_ref.shape
    tiles = [tile_of(slot, info) for slot in slots]
    swaps = [info[1 + tile] != info[0] for tile in tiles]

    def copy(index, channel):
        turn = lax.rem(channel, 2)
        return pltpu.make_async_copy(
            held.at[turn, index], out_ref.at[tiles[index], first + channel], sems.at[turn, index]
        )

    def one_channel(channel, _):
        turn = lax.rem(channel, 2)

        @pl.when(channel >= 2)
        def _():
            for index in range(count):
                copy(index, channel - 2).wait()

        own = [split(own_ref[channel, part]) for part in range(2)]
        for index in range(count):
            if slots[index][0] == "own":
                left = right = own
            else:
                far = [split(far_refs[index][channel, part]) for part in range(2)]
                swapped = swaps[index]
                left = [[jnp.where(swapped, f, o) for f, o in zip(a, b)] for a, b in zip(far, own)]
                right = [[jnp.where(swapped, o, f) for f, o in zip(a, b)] for a, b in zip(far, own)]
            rows_high = jnp.concatenate([left[0][0], left[1][0]], axis=1)
            rows_low = jnp.concatenate([left[0][1], left[1][1]], axis=1)
            columns = []
            for level in range(2):
                real = jnp.concatenate([right[0][level], right[1][level]], axis=1)
                imag = jnp.concatenate([-right[1][level], right[0][level]], axis=1)
                columns.append(jnp.concatenate([real, imag], axis=0))
            dims = (((1,), (1,)), ((), ()))
            both = lax.dot_general(
                jnp.concatenate([rows_high, rows_low], axis=0),
                columns[0],
                dims,
                preferred_element_type=jnp.float32,
            )
            cross = lax.dot_general(rows_high, columns[1], dims, preferred_element_type=jnp.float32)
            total = (both[:width] + (both[width:] + cross)) * (1.0 / samples)
            held[turn, index, 0] = total[:, :width]
            held[turn, index, 1] = total[:, width:]
            copy(index, channel).start()
        return 0

    lax.fori_loop(0, channels, one_channel, 0)
    for channel in range(max(0, channels - 2), channels):
        for index in range(count):
            copy(index, channel).wait()


def correlate(visibility, shape, info, own, fars, slots, first, name):
    count = len(slots)
    channels, parts, width, samples = own.shape
    inside = pl.BlockSpec(memory_space=pltpu.VMEM)
    anywhere = pl.BlockSpec(memory_space=pl.ANY)
    before = [] if visibility is None else [visibility]
    return pl.pallas_call(
        functools.partial(tiles_kernel, slots, first),
        in_specs=[pl.BlockSpec(memory_space=pltpu.SMEM)] + [inside] * (len(fars) + 1) + [anywhere] * len(before),
        out_specs=anywhere,
        scratch_shapes=[
            pltpu.VMEM((2, count, 2, width, width), jnp.float32),
            pltpu.SemaphoreType.DMA((2, count)),
        ],
        out_shape=jax.ShapeDtypeStruct(shape, jnp.float32),
        input_output_aliases={len(fars) + 2: 0} if before else {},
        compiler_params=pltpu.CompilerParams(vmem_limit_bytes=16 * 1024 * 1024),
        cost_estimate=pl.CostEstimate(
            flops=channels * count * 2 * 3 * width * 2 * width * samples * 2,
            bytes_accessed=4 * channels * parts * width * ((len(fars) + 1) * samples + count * width),
            transcendentals=0,
        ),
        name=name,
    )(info, own, *fars, *before)


def gather_kernel(info, *refs):
    pieces, out_ref = refs[:SIDE], refs[SIDE]
    rows = pieces[0].shape[2]
    for shift in range(SIDE):
        source = lax.rem(info[0] + SIDE - shift, SIDE)
        start = pl.multiple_of(source * rows, rows)
        out_ref[:, :, pl.ds(start, rows)] = pieces[shift][...]


def on_chip(kernel, info, values, shapes, name):
    inside = pl.BlockSpec(memory_space=pltpu.VMEM)
    return pl.pallas_call(
        kernel,
        in_specs=[pl.BlockSpec(memory_space=pltpu.SMEM)] + [inside] * len(values),
        out_specs=[inside] * len(shapes),
        out_shape=[jax.ShapeDtypeStruct(shape, jnp.float32) for shape in shapes],
        compiler_params=pltpu.CompilerParams(vmem_limit_bytes=16 * 1024 * 1024),
        name=name,
    )(info, *values)


def gather_rows(info, pieces):
    count, parts, rows, samples = pieces[0].shape
    return on_chip(gather_kernel, info, pieces, [(count, parts, rows * SIDE, samples)], "rows")[0]


def choose_kernel(rule, info, first_ref, second_ref, *outs):
    for out, wanted in zip(outs, rule(*position(info))):

        @pl.when(wanted)
        def _():
            out[...] = first_ref[...]

        @pl.when(jnp.logical_not(wanted))
        def _():
            out[...] = second_ref[...]


def choose(rule, count, info, first, second, name):
    return on_chip(functools.partial(choose_kernel, rule), info, [first, second], [first.shape] * count, name)


def far_column(z, core):
    return [z >= 2]


def row_sources(z, core):
    down = z >= 1
    up = z == SIDE - 1
    first = core == 0
    return [jnp.where(first, down, up), jnp.where(first, up, down), core == 1]


def shards(voltages, pair_table, bad_feeds):
    here = lax.axis_index("blk").astype(jnp.int32)
    freq = lax.axis_index("freq").astype(jnp.int32)
    freq_count = lax.axis_size("freq")
    _, channels, parts, rows, samples = voltages.shape
    group = channels // freq_count
    width = rows * freq_count

    inputs = here * width + freq * rows + jnp.arange(rows, dtype=jnp.int32)
    flagged = jnp.any((inputs // 2)[:, None] == bad_feeds[None, :], axis=-1)
    keep = jnp.where(flagged, 0.0, 1.0).astype(jnp.float32)[:, None]
    info = jnp.concatenate([here[None], pair_table[:, 0]])
    freq_info = freq[None]
    shape = (pair_table.shape[0], group, parts, width, width)
    firsts = [sum(CHUNKS[:number]) for number in range(len(CHUNKS))]

    def corner_turn(number, *earlier):
        count = CHUNKS[number]
        with jax.named_scope(f"turn_{number}"):

            def piece(shift):
                start = ((freq + shift) % freq_count) * group + firsts[number]
                return lax.dynamic_slice_in_dim(voltages[0], start, count, 0) * keep

            pieces = [piece(0)]
            for shift in (1, 2, 3):
                pairs = [(source, (source + shift) % freq_count) for source in range(freq_count)]
                pieces.append(lax.ppermute(after(piece(shift), *earlier), "freq", pairs))
            return gather_rows(freq_info, pieces)

    def scoped(name, number, value, source_of):
        with jax.named_scope(f"{name}_{number}"):
            return fetch(value, source_of)

    def exchange(name, number, value):
        return scoped(name + "_core", number, value, lambda x, z, c: (x, z, 1 - c))

    def get_q0(number, own, *earlier):
        own = after(own, *earlier)
        q0 = scoped("q0", number, own, lambda x, z, c: (x + 1, z, c))
        w = scoped("w", number, own, lambda x, z, c: (x - 1, z, c) if z >= 2 else None)
        return q0, w

    def get_row(number, q0, *earlier):
        q0 = after(q0, *earlier)
        qa = scoped("qa", number, q0, lambda x, z, c: (x, z + side(c, False), c))
        qb = scoped("qb", number, q0, lambda x, z, c: (x, z + side(c, True), c))
        return qa, qb

    def get_q2(number, qa, *earlier):
        return scoped("q2", number, after(qa, *earlier), lambda x, z, c: (x, z + side(c, False), c))

    def get_rc(number, q0, w, *earlier):
        source = choose(far_column, 1, info, after(w, *earlier), q0, f"pick_{number}")[0]
        return scoped(
            "rc", number, source, lambda x, z, c: (x - 1, z, c) if z >= 2 else (x + 1, z, c)
        )

    def get_s(number, own, rc, *earlier):
        to_a, to_b, to_mixed = choose(row_sources, 3, info, own, rc, f"pick3_{number}")
        sa = scoped("sa", number, to_a, lambda x, z, c: (x, z + side(c, False), c))
        sb = scoped("sb", number, after(to_b, *earlier), lambda x, z, c: (x, z + side(c, True), c))
        return sa, sb, exchange("rc", number, to_mixed)

    def get_x2(number, q2, *earlier):
        return scoped(
            "x2", number, after(q2, *earlier), lambda x, z, c: (x - 1, z, c) if z <= 1 else (x + 1, z, c)
        )

    def tiles(visibility, number, own, fars, slots, label):
        return correlate(
            visibility, shape, info, own, fars, slots, firsts[number], f"tiles_{label}_{number}"
        )

    near = ("ahead", 1, 3)
    away = ("ahead", 3, 1)
    same = ("ahead", 0, 0)
    twice = ("ahead", 2, 2)

    def with_other(slot):
        return [(*slot, False), (*slot, True)]

    def group_1(visibility, number, own, q0, q0_other):
        slots = with_other(same) + [("own", 0, 0, False)]
        return tiles(visibility, number, own, [q0, q0_other], slots, "g1")

    def group_2(visibility, number, own, qa, qa_other, qb, qb_other):
        slots = with_other(near) + with_other(away)
        return tiles(visibility, number, own, [qa, qa_other, qb, qb_other], slots, "g2")

    def group_3(visibility, number, own, rc, mixed, q2, q2_other):
        slots = [("two", 0, 0, False), ("mixed", 0, 0, False)] + with_other(twice)
        return tiles(visibility, number, own, [rc, mixed, q2, q2_other], slots, "g3")

    def group_4(visibility, number, own, sa, sa_other, sb, sb_other):
        slots = with_other(("row", 1, 3)) + with_other(("row", 3, 1))
        return tiles(visibility, number, own, [sa, sa_other, sb, sb_other], slots, "g4")

    def group_5(visibility, number, own, x2, x2_other):
        return tiles(visibility, number, own, [x2, x2_other], with_other(("row", 2, 2)), "g5")

    own_0 = corner_turn(0)
    q0_0, w_0 = get_q0(0, own_0)
    own_1 = corner_turn(1, own_0)
    qa_0, qb_0 = get_row(0, q0_0, own_1)
    rc_0 = get_rc(0, q0_0, w_0)
    q0_0x = exchange("q0", 0, q0_0)
    q2_0 = get_q2(0, qa_0)
    vis = group_1(None, 0, own_0, q0_0, q0_0x)
    q0_1, w_1 = get_q0(1, own_1, rc_0)
    sa_0, sb_0, mixed_0 = get_s(0, own_0, rc_0, q2_0, vis)
    qa_0x = exchange("qa", 0, qa_0)
    qb_0x = exchange("qb", 0, qb_0)
    q2_0x = exchange("q2", 0, q2_0)
    vis = group_2(vis, 0, own_0, qa_0, qa_0x, qb_0, qb_0x)
    qa_1, qb_1 = get_row(1, q0_1, sa_0, sb_0, vis)
    rc_1 = get_rc(1, q0_1, w_1)
    x2_0 = get_x2(0, q2_0, q0_1)
    q0_1x = exchange("q0", 1, q0_1)
    vis = group_3(vis, 0, own_0, rc_0, mixed_0, q2_0, q2_0x)
    sa_0x = exchange("sa", 0, sa_0)
    sb_0x = exchange("sb", 0, sb_0)
    q2_1 = get_q2(1, qa_1, vis)
    vis = group_1(vis, 1, own_1, q0_1, q0_1x)
    vis = group_4(vis, 0, own_0, sa_0, sa_0x, sb_0, sb_0x)
    sa_1, sb_1, mixed_1 = get_s(1, own_1, rc_1, q2_1, vis)
    qa_1x = exchange("qa", 1, qa_1)
    qb_1x = exchange("qb", 1, qb_1)
    x2_0x = exchange("x2", 0, x2_0)
    x2_1 = get_x2(1, q2_1)
    q2_1x = exchange("q2", 1, q2_1)
    vis = group_5(vis, 0, own_0, x2_0, x2_0x)
    vis = group_2(vis, 1, own_1, qa_1, qa_1x, qb_1, qb_1x)
    vis = group_3(vis, 1, own_1, rc_1, mixed_1, q2_1, q2_1x)
    sa_1x = exchange("sa", 1, after(sa_1, vis))
    sb_1x = exchange("sb", 1, sb_1)
    vis = group_4(vis, 1, own_1, sa_1, sa_1x, sb_1, sb_1x)
    x2_1x = exchange("x2", 1, x2_1)
    return group_5(vis, 1, own_1, x2_1, x2_1x)


def solution(mesh):
    placed = (P("blk", None, None, "freq", None), P("blk", None), P())
    return jax.shard_map(
        shards,
        mesh=mesh,
        in_specs=placed,
        out_specs=P("blk", "freq", None, None, None),
        check_vma=False,
    )
```

```python
import functools

import jax
import jax.numpy as jnp
from jax import lax
from jax.experimental import pallas as pl
from jax.experimental.pallas import tpu as pltpu
from jax.sharding import PartitionSpec as P

CHUNKS = (4, 4)
SIDE = 4

ORDER = (('own', 0), ('q0', 0), ('w', 0), ('own', 1), ('qa', 0), ('qb', 0), ('rc', 0), ('q0x', 0), ('tiles', 0), ('q2', 0), ('q0', 1), ('w', 1), ('qax', 0), ('qbx', 0), ('tiles', 1), ('sa', 0), ('sb', 0), ('rcx', 0), ('q2x', 0), ('tiles', 2), ('qa', 1), ('x2', 0), ('q0x', 1), ('qb', 1), ('tiles', 3), ('rc', 1), ('q2', 1), ('sax', 0), ('sbx', 0), ('tiles', 4), ('x2x', 0), ('qax', 1), ('qbx', 1), ('sa', 1), ('sb', 1), ('rcx', 1), ('x2', 1), ('q2x', 1), ('tiles', 5), ('tiles', 6), ('tiles', 7), ('sax', 1), ('sbx', 1), ('tiles', 8), ('x2x', 1), ('tiles', 9))
LATER = {('own', 1): (('own', 0),), ('qa', 0): (('own', 1),), ('qb', 0): (('own', 1),), ('q2', 0): (('tiles', 0),), ('q0', 1): (('rc', 0), ('tiles', 0)), ('w', 1): (('tiles', 0),), ('sb', 0): (('q2', 0), ('tiles', 1), ('w', 1)), ('qa', 1): (('tiles', 2), ('w', 1)), ('x2', 0): (('q0', 1), ('tiles', 2)), ('qb', 1): (('sa', 0), ('tiles', 2)), ('q2', 1): (('tiles', 3),), ('x2x', 0): (('tiles', 4),), ('sb', 1): (('q2', 1), ('tiles', 4)), ('x2', 1): (('tiles', 4),), ('sax', 1): (('tiles', 7),), ('sbx', 1): (('tiles', 7),)}
KERNELS = ((0, ('q0', 'own')), (0, ('qa', 'qb')), (0, ('rc', 'q2')), (1, ('q0', 'own')), (0, ('sa', 'sb')), (0, ('x2',)), (1, ('qa', 'qb')), (1, ('rc', 'q2')), (1, ('sa', 'sb')), (1, ('x2',)))


def place(x, z, core):
    return ((x % SIDE) * SIDE + z % SIDE) * 2 + core


def fetch(value, source_of):
    pairs = []
    for x in range(SIDE):
        for z in range(SIDE):
            for core in range(2):
                source = source_of(x, z, core)
                if source is not None:
                    pairs.append((place(*source), place(x, z, core)))
    return lax.ppermute(value, "blk", pairs)


def side(core, flip):
    return 1 if (core == 0) != flip else -1


def after(value, *others):
    return lax.optimization_barrier((value, *others))[0]


def position(info):
    here = info[0]
    return lax.rem(lax.div(here, 2), SIDE), lax.rem(here, 2)


def tile_of(slot, info):
    kind, distance_0, distance_1, exchanged = slot
    z, core = position(info)
    if kind == "own":
        return jnp.int32(0)
    if kind == "mixed":
        return jnp.where(core == 0, 1, 15)
    mine = jnp.where(core == 0, distance_0, distance_1)
    other = jnp.where(core == 0, distance_1, distance_0)
    distance = other if exchanged else mine
    wraps = z + distance >= SIDE
    if kind == "ahead":
        chips = jnp.where(wraps, distance, distance + SIDE)
    else:
        chips = jnp.where(wraps, distance + SIDE, distance)
    if kind == "two":
        chips = jnp.int32(2 * SIDE)
    if exchanged:
        return jnp.where(core == 0, 2 * chips + 1, 2 * chips - 1)
    return 2 * chips


def split(value):
    high = value.astype(jnp.bfloat16)
    low = (value - high.astype(jnp.float32)).astype(jnp.bfloat16)
    return high, low


def tiles_kernel(slots, first, info, own_ref, *refs):
    count = len(slots)
    far_refs = refs[: count - sum(slot[0] == "own" for slot in slots)]
    out_ref, held, sems = refs[-3:]
    channels, _, width, samples = own_ref.shape
    tiles = [tile_of(slot, info) for slot in slots]
    swaps = [info[1 + tile] != info[0] for tile in tiles]

    def copy(index, channel):
        turn = lax.rem(channel, 2)
        return pltpu.make_async_copy(
            held.at[turn, index], out_ref.at[tiles[index], first + channel], sems.at[turn, index]
        )

    def one_channel(channel, _):
        turn = lax.rem(channel, 2)

        @pl.when(channel >= 2)
        def _():
            for index in range(count):
                copy(index, channel - 2).wait()

        own = [split(own_ref[channel, part]) for part in range(2)]
        for index in range(count):
            if slots[index][0] == "own":
                left = right = own
            else:
                far = [split(far_refs[index][channel, part]) for part in range(2)]
                swapped = swaps[index]
                left = [[jnp.where(swapped, f, o) for f, o in zip(a, b)] for a, b in zip(far, own)]
                right = [[jnp.where(swapped, o, f) for f, o in zip(a, b)] for a, b in zip(far, own)]
            rows_high = jnp.concatenate([left[0][0], left[1][0]], axis=1)
            rows_low = jnp.concatenate([left[0][1], left[1][1]], axis=1)
            columns = []
            for level in range(2):
                real = jnp.concatenate([right[0][level], right[1][level]], axis=1)
                imag = jnp.concatenate([-right[1][level], right[0][level]], axis=1)
                columns.append(jnp.concatenate([real, imag], axis=0))
            dims = (((1,), (1,)), ((), ()))
            both = lax.dot_general(
                jnp.concatenate([rows_high, rows_low], axis=0),
                columns[0],
                dims,
                preferred_element_type=jnp.float32,
            )
            cross = lax.dot_general(rows_high, columns[1], dims, preferred_element_type=jnp.float32)
            total = (both[:width] + (both[width:] + cross)) * (1.0 / samples)
            held[turn, index, 0] = total[:, :width]
            held[turn, index, 1] = total[:, width:]
            copy(index, channel).start()
        return 0

    lax.fori_loop(0, channels, one_channel, 0)
    for channel in range(max(0, channels - 2), channels):
        for index in range(count):
            copy(index, channel).wait()


def correlate(visibility, shape, info, own, fars, slots, first, name):
    count = len(slots)
    channels, parts, width, samples = own.shape
    inside = pl.BlockSpec(memory_space=pltpu.VMEM)
    anywhere = pl.BlockSpec(memory_space=pl.ANY)
    before = [] if visibility is None else [visibility]
    return pl.pallas_call(
        functools.partial(tiles_kernel, slots, first),
        in_specs=[pl.BlockSpec(memory_space=pltpu.SMEM)] + [inside] * (len(fars) + 1) + [anywhere] * len(before),
        out_specs=anywhere,
        scratch_shapes=[
            pltpu.VMEM((2, count, 2, width, width), jnp.float32),
            pltpu.SemaphoreType.DMA((2, count)),
        ],
        out_shape=jax.ShapeDtypeStruct(shape, jnp.float32),
        input_output_aliases={len(fars) + 2: 0} if before else {},
        compiler_params=pltpu.CompilerParams(vmem_limit_bytes=16 * 1024 * 1024),
        cost_estimate=pl.CostEstimate(
            flops=channels * count * 2 * 3 * width * 2 * width * samples * 2,
            bytes_accessed=4 * channels * parts * width * ((len(fars) + 1) * samples + count * width),
            transcendentals=0,
        ),
        name=name,
    )(info, own, *fars, *before)


def gather_kernel(info, *refs):
    pieces, keep_ref, out_ref = refs[:SIDE], refs[SIDE], refs[SIDE + 1]
    rows = pieces[0].shape[2]
    for shift in range(SIDE):
        source = lax.rem(info[0] + SIDE - shift, SIDE)
        start = pl.multiple_of(source * rows, rows)
        out_ref[:, :, pl.ds(start, rows)] = pieces[shift][...] * keep_ref[pl.ds(start, rows)]


def on_chip(kernel, info, values, shapes, name):
    inside = pl.BlockSpec(memory_space=pltpu.VMEM)
    return pl.pallas_call(
        kernel,
        in_specs=[pl.BlockSpec(memory_space=pltpu.SMEM)] + [inside] * len(values),
        out_specs=[inside] * len(shapes),
        out_shape=[jax.ShapeDtypeStruct(shape, jnp.float32) for shape in shapes],
        compiler_params=pltpu.CompilerParams(vmem_limit_bytes=16 * 1024 * 1024),
        name=name,
    )(info, *values)


def gather_rows(info, pieces, keep):
    count, parts, rows, samples = pieces[0].shape
    return on_chip(gather_kernel, info, [*pieces, keep], [(count, parts, rows * SIDE, samples)], "rows")[0]


def choose_kernel(rule, info, first_ref, second_ref, *outs):
    for out, wanted in zip(outs, rule(*position(info))):

        @pl.when(wanted)
        def _():
            out[...] = first_ref[...]

        @pl.when(jnp.logical_not(wanted))
        def _():
            out[...] = second_ref[...]


def choose(rule, count, info, first, second, name):
    return on_chip(functools.partial(choose_kernel, rule), info, [first, second], [first.shape] * count, name)


def far_column(z, core):
    return [z >= 2]


def row_sources(z, core):
    down = z >= 1
    up = z == SIDE - 1
    first = core == 0
    return [jnp.where(first, down, up), jnp.where(first, up, down), core == 1]


KINDS = {
    "q0": ("ahead", 0, 0),
    "qa": ("ahead", 1, 3),
    "qb": ("ahead", 3, 1),
    "q2": ("ahead", 2, 2),
    "rc": ("two", 0, 0),
    "sa": ("row", 1, 3),
    "sb": ("row", 3, 1),
    "x2": ("row", 2, 2),
}
PATHS = {
    "q0": lambda x, z, c: (x + 1, z, c),
    "w": lambda x, z, c: (x - 1, z, c) if z >= 2 else None,
    "rc": lambda x, z, c: (x - 1, z, c) if z >= 2 else (x + 1, z, c),
    "qa": lambda x, z, c: (x, z + side(c, False), c),
    "qb": lambda x, z, c: (x, z + side(c, True), c),
    "q2": lambda x, z, c: (x, z + side(c, False), c),
    "sa": lambda x, z, c: (x, z + side(c, False), c),
    "sb": lambda x, z, c: (x, z + side(c, True), c),
    "x2": lambda x, z, c: (x - 1, z, c) if z <= 1 else (x + 1, z, c),
}


def other_core(x, z, c):
    return x, z, 1 - c


def shards(voltages, pair_table, bad_feeds):
    here = lax.axis_index("blk").astype(jnp.int32)
    freq = lax.axis_index("freq").astype(jnp.int32)
    freq_count = lax.axis_size("freq")
    _, channels, parts, rows, samples = voltages.shape
    group = channels // freq_count
    width = rows * freq_count

    inputs = here * width + jnp.arange(width, dtype=jnp.int32)
    flagged = jnp.any((inputs // 2)[:, None] == bad_feeds[None, :], axis=-1)
    keep = jnp.where(flagged, 0.0, 1.0).astype(jnp.float32)[:, None]
    keep = jnp.broadcast_to(keep, (width, samples))
    info = jnp.concatenate([here[None], pair_table[:, 0]])
    shape = (pair_table.shape[0], group, parts, width, width)
    firsts = [sum(CHUNKS[:number]) for number in range(len(CHUNKS))]
    done = {}
    picked = {}

    def corner_turn(number, earlier):
        count = CHUNKS[number]

        def piece(shift):
            start = ((freq + shift) % freq_count) * group + firsts[number]
            return lax.dynamic_slice_in_dim(voltages[0], start, count, 0)

        pieces = [piece(0)]
        for shift in (1, 2, 3):
            pairs = [(source, (source + shift) % freq_count) for source in range(freq_count)]
            pieces.append(lax.ppermute(after(piece(shift), *earlier), "freq", pairs))
        return gather_rows(freq[None], pieces, keep)

    def pick(number):
        if number not in picked:
            picked[number] = choose(
                row_sources, 3, info, done["own", number], done["rc", number], f"pick3_{number}"
            )
        return picked[number]

    def tiles(visibility, index, number, items):
        slots, fars = [], []
        for name in items:
            if name == "own":
                slots.append(("own", 0, 0, False))
                continue
            slots.append((*KINDS[name], False))
            fars.append(done[name, number])
            slots.append(("mixed", 0, 0, False) if name == "rc" else (*KINDS[name], True))
            fars.append(done[name + "x", number])
        slots.sort(key=lambda slot: slot[0] == "own")
        return correlate(
            visibility, shape, info, done["own", number], fars, slots, firsts[number], f"tiles_k{index}"
        )

    def step(name, number):
        earlier = [done[other] for other in LATER.get((name, number), ())]
        if name == "own":
            return corner_turn(number, earlier)
        if name == "rc":
            value = choose(far_column, 1, info, done["w", number], done["q0", number], f"pick_{number}")[0]
        elif name in ("sa", "sb", "rcx"):
            value = pick(number)[("sa", "sb", "rcx").index(name)]
        elif name.endswith("x") and name != "x2":
            value = done[name[:-1], number]
        else:
            value = done[{"q0": "own", "w": "own", "qa": "q0", "qb": "q0", "q2": "qa", "x2": "q2"}[name], number]
        return fetch(after(value, *earlier), PATHS.get(name, other_core))

    visibility = None
    for name, number in ORDER:
        with jax.named_scope(f"n_{name}_{number}"):
            if name == "tiles":
                visibility = tiles(visibility, number, *KERNELS[number])
                done[name, number] = visibility
            else:
                done[name, number] = step(name, number)
    return visibility


def solution(mesh):
    placed = (P("blk", None, None, "freq", None), P("blk", None), P())
    return jax.shard_map(
        shards,
        mesh=mesh,
        in_specs=placed,
        out_specs=P("blk", "freq", None, None, None),
        check_vma=False,
    )
```

```python
import functools

import jax
import jax.numpy as jnp
from jax import lax
from jax.experimental import pallas as pl
from jax.experimental.pallas import tpu as pltpu
from jax.sharding import PartitionSpec as P

CHUNKS = (4, 4)
SIDE = 4

ORDER = (('own', 0), ('q0', 0), ('w', 0), ('own', 1), ('qa', 0), ('qb', 0), ('rc', 0), ('q0x', 0), ('tiles', 0), ('q2', 0), ('q0', 1), ('w', 1), ('qax', 0), ('qbx', 0), ('tiles', 1), ('sa', 0), ('sb', 0), ('rcx', 0), ('q2x', 0), ('tiles', 2), ('qa', 1), ('q0x', 1), ('qb', 1), ('tiles', 3), ('x2', 0), ('rc', 1), ('q2', 1), ('sax', 0), ('sbx', 0), ('tiles', 4), ('x2x', 0), ('qax', 1), ('qbx', 1), ('sa', 1), ('sb', 1), ('rcx', 1), ('x2', 1), ('q2x', 1), ('tiles', 5), ('tiles', 6), ('tiles', 7), ('sax', 1), ('sbx', 1), ('tiles', 8), ('x2x', 1), ('tiles', 9))
LATER = {('own', 1): (('own', 0),), ('qa', 0): (('own', 1),), ('qb', 0): (('own', 1),), ('q2', 0): (('tiles', 0),), ('q0', 1): (('rc', 0), ('tiles', 0)), ('w', 1): (('tiles', 0),), ('sb', 0): (('q2', 0), ('tiles', 1), ('w', 1)), ('qa', 1): (('tiles', 2), ('w', 1)), ('x2', 0): (('q0', 1), ('tiles', 3)), ('qb', 1): (('sa', 0), ('tiles', 2)), ('q2', 1): (('tiles', 3),), ('x2x', 0): (('tiles', 4),), ('sb', 1): (('q2', 1), ('tiles', 4)), ('x2', 1): (('tiles', 4),), ('sax', 1): (('tiles', 7),), ('sbx', 1): (('tiles', 7),)}
KERNELS = ((0, ('q0', 'own')), (0, ('qa', 'qb')), (0, ('rc', 'q2')), (1, ('q0', 'own')), (0, ('sa', 'sb')), (0, ('x2',)), (1, ('qa', 'qb')), (1, ('rc', 'q2')), (1, ('sa', 'sb')), (1, ('x2',)))


def place(x, z, core):
    return ((x % SIDE) * SIDE + z % SIDE) * 2 + core


def fetch(value, source_of):
    pairs = []
    for x in range(SIDE):
        for z in range(SIDE):
            for core in range(2):
                source = source_of(x, z, core)
                if source is not None:
                    pairs.append((place(*source), place(x, z, core)))
    return lax.ppermute(value, "blk", pairs)


def side(core, flip):
    return 1 if (core == 0) != flip else -1


def after(value, *others):
    return lax.optimization_barrier((value, *others))[0]


def position(info):
    here = info[0]
    return lax.rem(lax.div(here, 2), SIDE), lax.rem(here, 2)


def tile_of(slot, info):
    kind, distance_0, distance_1, exchanged = slot
    z, core = position(info)
    if kind == "own":
        return jnp.int32(0)
    if kind == "mixed":
        return jnp.where(core == 0, 1, 15)
    mine = jnp.where(core == 0, distance_0, distance_1)
    other = jnp.where(core == 0, distance_1, distance_0)
    distance = other if exchanged else mine
    wraps = z + distance >= SIDE
    if kind == "ahead":
        chips = jnp.where(wraps, distance, distance + SIDE)
    else:
        chips = jnp.where(wraps, distance + SIDE, distance)
    if kind == "two":
        chips = jnp.int32(2 * SIDE)
    if exchanged:
        return jnp.where(core == 0, 2 * chips + 1, 2 * chips - 1)
    return 2 * chips


def split(value):
    high = value.astype(jnp.bfloat16)
    low = (value - high.astype(jnp.float32)).astype(jnp.bfloat16)
    return high, low


def tiles_kernel(slots, first, info, own_ref, *refs):
    count = len(slots)
    far_refs = refs[: count - sum(slot[0] == "own" for slot in slots)]
    out_ref, held, sems = refs[-3:]
    channels, _, width, samples = own_ref.shape
    tiles = [tile_of(slot, info) for slot in slots]
    swaps = [info[1 + tile] != info[0] for tile in tiles]

    def copy(index, channel):
        turn = lax.rem(channel, 2)
        return pltpu.make_async_copy(
            held.at[turn, index], out_ref.at[tiles[index], first + channel], sems.at[turn, index]
        )

    def one_channel(channel, _):
        turn = lax.rem(channel, 2)

        @pl.when(channel >= 2)
        def _():
            for index in range(count):
                copy(index, channel - 2).wait()

        own = [split(own_ref[channel, part]) for part in range(2)]
        for index in range(count):
            if slots[index][0] == "own":
                left = right = own
            else:
                far = [split(far_refs[index][channel, part]) for part in range(2)]
                swapped = swaps[index]
                left = [[jnp.where(swapped, f, o) for f, o in zip(a, b)] for a, b in zip(far, own)]
                right = [[jnp.where(swapped, o, f) for f, o in zip(a, b)] for a, b in zip(far, own)]
            rows_high = jnp.concatenate([left[0][0], left[1][0]], axis=1)
            rows_low = jnp.concatenate([left[0][1], left[1][1]], axis=1)
            columns = []
            for level in range(2):
                real = jnp.concatenate([right[0][level], right[1][level]], axis=1)
                imag = jnp.concatenate([-right[1][level], right[0][level]], axis=1)
                columns.append(jnp.concatenate([real, imag], axis=0))
            dims = (((1,), (1,)), ((), ()))
            both = lax.dot_general(
                jnp.concatenate([rows_high, rows_low], axis=0),
                columns[0],
                dims,
                preferred_element_type=jnp.float32,
            )
            cross = lax.dot_general(rows_high, columns[1], dims, preferred_element_type=jnp.float32)
            total = (both[:width] + (both[width:] + cross)) * (1.0 / samples)
            held[turn, index, 0] = total[:, :width]
            held[turn, index, 1] = total[:, width:]
            copy(index, channel).start()
        return 0

    lax.fori_loop(0, channels, one_channel, 0)
    for channel in range(max(0, channels - 2), channels):
        for index in range(count):
            copy(index, channel).wait()


def correlate(visibility, shape, info, own, fars, slots, first, name):
    count = len(slots)
    channels, parts, width, samples = own.shape
    inside = pl.BlockSpec(memory_space=pltpu.VMEM)
    anywhere = pl.BlockSpec(memory_space=pl.ANY)
    before = [] if visibility is None else [visibility]
    return pl.pallas_call(
        functools.partial(tiles_kernel, slots, first),
        in_specs=[pl.BlockSpec(memory_space=pltpu.SMEM)] + [inside] * (len(fars) + 1) + [anywhere] * len(before),
        out_specs=anywhere,
        scratch_shapes=[
            pltpu.VMEM((2, count, 2, width, width), jnp.float32),
            pltpu.SemaphoreType.DMA((2, count)),
        ],
        out_shape=jax.ShapeDtypeStruct(shape, jnp.float32),
        input_output_aliases={len(fars) + 2: 0} if before else {},
        compiler_params=pltpu.CompilerParams(vmem_limit_bytes=16 * 1024 * 1024),
        cost_estimate=pl.CostEstimate(
            flops=channels * count * 2 * 3 * width * 2 * width * samples * 2,
            bytes_accessed=4 * channels * parts * width * ((len(fars) + 1) * samples + count * width),
            transcendentals=0,
        ),
        name=name,
    )(info, own, *fars, *before)


def gather_kernel(info, *refs):
    pieces, keep_ref, out_ref = refs[:SIDE], refs[SIDE], refs[SIDE + 1]
    rows = pieces[0].shape[2]
    for shift in range(SIDE):
        source = lax.rem(info[0] + SIDE - shift, SIDE)
        start = pl.multiple_of(source * rows, rows)
        out_ref[:, :, pl.ds(start, rows)] = pieces[shift][...] * keep_ref[pl.ds(start, rows)]


def on_chip(kernel, info, values, shapes, name):
    inside = pl.BlockSpec(memory_space=pltpu.VMEM)
    return pl.pallas_call(
        kernel,
        in_specs=[pl.BlockSpec(memory_space=pltpu.SMEM)] + [inside] * len(values),
        out_specs=[inside] * len(shapes),
        out_shape=[jax.ShapeDtypeStruct(shape, jnp.float32) for shape in shapes],
        compiler_params=pltpu.CompilerParams(vmem_limit_bytes=16 * 1024 * 1024),
        name=name,
    )(info, *values)


def gather_rows(info, pieces, keep):
    count, parts, rows, samples = pieces[0].shape
    return on_chip(gather_kernel, info, [*pieces, keep], [(count, parts, rows * SIDE, samples)], "rows")[0]


def choose_kernel(rule, info, first_ref, second_ref, *outs):
    for out, wanted in zip(outs, rule(*position(info))):

        @pl.when(wanted)
        def _():
            out[...] = first_ref[...]

        @pl.when(jnp.logical_not(wanted))
        def _():
            out[...] = second_ref[...]


def choose(rule, count, info, first, second, name):
    return on_chip(functools.partial(choose_kernel, rule), info, [first, second], [first.shape] * count, name)


def far_column(z, core):
    return [z >= 2]


def row_sources(z, core):
    down = z >= 1
    up = z == SIDE - 1
    first = core == 0
    return [jnp.where(first, down, up), jnp.where(first, up, down), core == 1]


KINDS = {
    "q0": ("ahead", 0, 0),
    "qa": ("ahead", 1, 3),
    "qb": ("ahead", 3, 1),
    "q2": ("ahead", 2, 2),
    "rc": ("two", 0, 0),
    "sa": ("row", 1, 3),
    "sb": ("row", 3, 1),
    "x2": ("row", 2, 2),
}
PATHS = {
    "q0": lambda x, z, c: (x + 1, z, c),
    "w": lambda x, z, c: (x - 1, z, c) if z >= 2 else None,
    "rc": lambda x, z, c: (x - 1, z, c) if z >= 2 else (x + 1, z, c),
    "qa": lambda x, z, c: (x, z + side(c, False), c),
    "qb": lambda x, z, c: (x, z + side(c, True), c),
    "q2": lambda x, z, c: (x, z + side(c, False), c),
    "sa": lambda x, z, c: (x, z + side(c, False), c),
    "sb": lambda x, z, c: (x, z + side(c, True), c),
    "x2": lambda x, z, c: (x - 1, z, c) if z <= 1 else (x + 1, z, c),
}


def other_core(x, z, c):
    return x, z, 1 - c


def shards(voltages, pair_table, bad_feeds):
    here = lax.axis_index("blk").astype(jnp.int32)
    freq = lax.axis_index("freq").astype(jnp.int32)
    freq_count = lax.axis_size("freq")
    _, channels, parts, rows, samples = voltages.shape
    group = channels // freq_count
    width = rows * freq_count

    inputs = here * width + jnp.arange(width, dtype=jnp.int32)
    flagged = jnp.any((inputs // 2)[:, None] == bad_feeds[None, :], axis=-1)
    keep = jnp.where(flagged, 0.0, 1.0).astype(jnp.float32)[:, None]
    keep = jnp.broadcast_to(keep, (width, samples))
    info = jnp.concatenate([here[None], pair_table[:, 0]])
    shape = (pair_table.shape[0], group, parts, width, width)
    firsts = [sum(CHUNKS[:number]) for number in range(len(CHUNKS))]
    done = {}
    picked = {}

    def corner_turn(number, earlier):
        count = CHUNKS[number]

        def piece(shift):
            start = ((freq + shift) % freq_count) * group + firsts[number]
            return lax.dynamic_slice_in_dim(voltages[0], start, count, 0)

        pieces = [piece(0)]
        for shift in (1, 2, 3):
            pairs = [(source, (source + shift) % freq_count) for source in range(freq_count)]
            pieces.append(lax.ppermute(after(piece(shift), *earlier), "freq", pairs))
        return gather_rows(freq[None], pieces, keep)

    def pick(number):
        if number not in picked:
            picked[number] = choose(
                row_sources, 3, info, done["own", number], done["rc", number], f"pick3_{number}"
            )
        return picked[number]

    def tiles(visibility, index, number, items):
        slots, fars = [], []
        for name in items:
            if name == "own":
                slots.append(("own", 0, 0, False))
                continue
            slots.append((*KINDS[name], False))
            fars.append(done[name, number])
            slots.append(("mixed", 0, 0, False) if name == "rc" else (*KINDS[name], True))
            fars.append(done[name + "x", number])
        slots.sort(key=lambda slot: slot[0] == "own")
        return correlate(
            visibility, shape, info, done["own", number], fars, slots, firsts[number], f"tiles_k{index}"
        )

    def step(name, number):
        earlier = [done[other] for other in LATER.get((name, number), ())]
        if name == "own":
            return corner_turn(number, earlier)
        if name == "rc":
            value = choose(far_column, 1, info, done["w", number], done["q0", number], f"pick_{number}")[0]
        elif name in ("sa", "sb", "rcx"):
            value = pick(number)[("sa", "sb", "rcx").index(name)]
        elif name.endswith("x") and name != "x2":
            value = done[name[:-1], number]
        else:
            value = done[{"q0": "own", "w": "own", "qa": "q0", "qb": "q0", "q2": "qa", "x2": "q2"}[name], number]
        return fetch(after(value, *earlier), PATHS.get(name, other_core))

    visibility = None
    for name, number in ORDER:
        with jax.named_scope(f"n_{name}_{number}"):
            if name == "tiles":
                visibility = tiles(visibility, number, *KERNELS[number])
                done[name, number] = visibility
            else:
                done[name, number] = step(name, number)
    return visibility


def solution(mesh):
    placed = (P("blk", None, None, "freq", None), P("blk", None), P())
    return jax.shard_map(
        shards,
        mesh=mesh,
        in_specs=placed,
        out_specs=P("blk", "freq", None, None, None),
        check_vma=False,
    )
```

```python
import functools

import jax
import jax.numpy as jnp
from jax import lax
from jax.experimental import pallas as pl
from jax.experimental.pallas import tpu as pltpu
from jax.sharding import PartitionSpec as P

CHUNKS = (4, 4)
SIDE = 4

ORDER = (('own', 0), ('q0', 0), ('w', 0), ('own', 1), ('qa', 0), ('qb', 0), ('rc', 0), ('q0x', 0), ('tiles', 0), ('q2', 0), ('q0', 1), ('w', 1), ('qax', 0), ('qbx', 0), ('tiles', 1), ('sa', 0), ('sb', 0), ('rcx', 0), ('q2x', 0), ('tiles', 2), ('qa', 1), ('q0x', 1), ('qb', 1), ('tiles', 3), ('rc', 1), ('q2', 1), ('sax', 0), ('x2', 0), ('sbx', 0), ('tiles', 4), ('x2x', 0), ('qax', 1), ('qbx', 1), ('sa', 1), ('sb', 1), ('rcx', 1), ('x2', 1), ('q2x', 1), ('tiles', 5), ('tiles', 6), ('tiles', 7), ('sax', 1), ('sbx', 1), ('tiles', 8), ('x2x', 1), ('tiles', 9))
LATER = {('own', 1): (('own', 0),), ('qa', 0): (('own', 1),), ('qb', 0): (('own', 1),), ('q2', 0): (('tiles', 0),), ('q0', 1): (('rc', 0), ('tiles', 0)), ('w', 1): (('tiles', 0),), ('sb', 0): (('q2', 0), ('tiles', 1), ('w', 1)), ('qa', 1): (('tiles', 2), ('w', 1)), ('x2', 0): (('q0', 1), ('tiles', 3), ('sax', 0)), ('qb', 1): (('sa', 0), ('tiles', 2)), ('q2', 1): (('tiles', 3),), ('x2x', 0): (('tiles', 4),), ('sb', 1): (('q2', 1), ('tiles', 4)), ('x2', 1): (('tiles', 4),), ('sax', 1): (('tiles', 7),), ('sbx', 1): (('tiles', 7),)}
KERNELS = ((0, ('q0', 'own')), (0, ('qa', 'qb')), (0, ('rc', 'q2')), (1, ('q0', 'own')), (0, ('sa', 'sb')), (0, ('x2',)), (1, ('qa', 'qb')), (1, ('rc', 'q2')), (1, ('sa', 'sb')), (1, ('x2',)))


def place(x, z, core):
    return ((x % SIDE) * SIDE + z % SIDE) * 2 + core


def fetch(value, source_of):
    pairs = []
    for x in range(SIDE):
        for z in range(SIDE):
            for core in range(2):
                source = source_of(x, z, core)
                if source is not None:
                    pairs.append((place(*source), place(x, z, core)))
    return lax.ppermute(value, "blk", pairs)


def side(core, flip):
    return 1 if (core == 0) != flip else -1


def after(value, *others):
    return lax.optimization_barrier((value, *others))[0]


def position(info):
    here = info[0]
    return lax.rem(lax.div(here, 2), SIDE), lax.rem(here, 2)


def tile_of(slot, info):
    kind, distance_0, distance_1, exchanged = slot
    z, core = position(info)
    if kind == "own":
        return jnp.int32(0)
    if kind == "mixed":
        return jnp.where(core == 0, 1, 15)
    mine = jnp.where(core == 0, distance_0, distance_1)
    other = jnp.where(core == 0, distance_1, distance_0)
    distance = other if exchanged else mine
    wraps = z + distance >= SIDE
    if kind == "ahead":
        chips = jnp.where(wraps, distance, distance + SIDE)
    else:
        chips = jnp.where(wraps, distance + SIDE, distance)
    if kind == "two":
        chips = jnp.int32(2 * SIDE)
    if exchanged:
        return jnp.where(core == 0, 2 * chips + 1, 2 * chips - 1)
    return 2 * chips


def split(value):
    high = value.astype(jnp.bfloat16)
    low = (value - high.astype(jnp.float32)).astype(jnp.bfloat16)
    return high, low


def tiles_kernel(slots, first, info, own_ref, *refs):
    count = len(slots)
    far_refs = refs[: count - sum(slot[0] == "own" for slot in slots)]
    out_ref, held, sems = refs[-3:]
    channels, _, width, samples = own_ref.shape
    tiles = [tile_of(slot, info) for slot in slots]
    swaps = [info[1 + tile] != info[0] for tile in tiles]

    def copy(index, channel):
        turn = lax.rem(channel, 2)
        return pltpu.make_async_copy(
            held.at[turn, index], out_ref.at[tiles[index], first + channel], sems.at[turn, index]
        )

    def one_channel(channel, _):
        turn = lax.rem(channel, 2)

        @pl.when(channel >= 2)
        def _():
            for index in range(count):
                copy(index, channel - 2).wait()

        own = [split(own_ref[channel, part]) for part in range(2)]
        for index in range(count):
            if slots[index][0] == "own":
                left = right = own
            else:
                far = [split(far_refs[index][channel, part]) for part in range(2)]
                swapped = swaps[index]
                left = [[jnp.where(swapped, f, o) for f, o in zip(a, b)] for a, b in zip(far, own)]
                right = [[jnp.where(swapped, o, f) for f, o in zip(a, b)] for a, b in zip(far, own)]
            rows_high = jnp.concatenate([left[0][0], left[1][0]], axis=1)
            rows_low = jnp.concatenate([left[0][1], left[1][1]], axis=1)
            columns = []
            for level in range(2):
                real = jnp.concatenate([right[0][level], right[1][level]], axis=1)
                imag = jnp.concatenate([-right[1][level], right[0][level]], axis=1)
                columns.append(jnp.concatenate([real, imag], axis=0))
            dims = (((1,), (1,)), ((), ()))
            both = lax.dot_general(
                jnp.concatenate([rows_high, rows_low], axis=0),
                columns[0],
                dims,
                preferred_element_type=jnp.float32,
            )
            cross = lax.dot_general(rows_high, columns[1], dims, preferred_element_type=jnp.float32)
            total = (both[:width] + (both[width:] + cross)) * (1.0 / samples)
            held[turn, index, 0] = total[:, :width]
            held[turn, index, 1] = total[:, width:]
            copy(index, channel).start()
        return 0

    lax.fori_loop(0, channels, one_channel, 0)
    for channel in range(max(0, channels - 2), channels):
        for index in range(count):
            copy(index, channel).wait()


def correlate(visibility, shape, info, own, fars, slots, first, name):
    count = len(slots)
    channels, parts, width, samples = own.shape
    inside = pl.BlockSpec(memory_space=pltpu.VMEM)
    anywhere = pl.BlockSpec(memory_space=pl.ANY)
    before = [] if visibility is None else [visibility]
    return pl.pallas_call(
        functools.partial(tiles_kernel, slots, first),
        in_specs=[pl.BlockSpec(memory_space=pltpu.SMEM)] + [inside] * (len(fars) + 1) + [anywhere] * len(before),
        out_specs=anywhere,
        scratch_shapes=[
            pltpu.VMEM((2, count, 2, width, width), jnp.float32),
            pltpu.SemaphoreType.DMA((2, count)),
        ],
        out_shape=jax.ShapeDtypeStruct(shape, jnp.float32),
        input_output_aliases={len(fars) + 2: 0} if before else {},
        compiler_params=pltpu.CompilerParams(vmem_limit_bytes=16 * 1024 * 1024),
        cost_estimate=pl.CostEstimate(
            flops=channels * count * 2 * 3 * width * 2 * width * samples * 2,
            bytes_accessed=4 * channels * parts * width * ((len(fars) + 1) * samples + count * width),
            transcendentals=0,
        ),
        name=name,
    )(info, own, *fars, *before)


def gather_kernel(info, *refs):
    pieces, keep_ref, out_ref = refs[:SIDE], refs[SIDE], refs[SIDE + 1]
    rows = pieces[0].shape[2]
    for shift in range(SIDE):
        source = lax.rem(info[0] + SIDE - shift, SIDE)
        start = pl.multiple_of(source * rows, rows)
        out_ref[:, :, pl.ds(start, rows)] = pieces[shift][...] * keep_ref[pl.ds(start, rows)]


def on_chip(kernel, info, values, shapes, name):
    inside = pl.BlockSpec(memory_space=pltpu.VMEM)
    return pl.pallas_call(
        kernel,
        in_specs=[pl.BlockSpec(memory_space=pltpu.SMEM)] + [inside] * len(values),
        out_specs=[inside] * len(shapes),
        out_shape=[jax.ShapeDtypeStruct(shape, jnp.float32) for shape in shapes],
        compiler_params=pltpu.CompilerParams(vmem_limit_bytes=16 * 1024 * 1024),
        name=name,
    )(info, *values)


def gather_rows(info, pieces, keep):
    count, parts, rows, samples = pieces[0].shape
    return on_chip(gather_kernel, info, [*pieces, keep], [(count, parts, rows * SIDE, samples)], "rows")[0]


def choose_kernel(rule, info, first_ref, second_ref, *outs):
    for out, wanted in zip(outs, rule(*position(info))):

        @pl.when(wanted)
        def _():
            out[...] = first_ref[...]

        @pl.when(jnp.logical_not(wanted))
        def _():
            out[...] = second_ref[...]


def choose(rule, count, info, first, second, name):
    return on_chip(functools.partial(choose_kernel, rule), info, [first, second], [first.shape] * count, name)


def far_column(z, core):
    return [z >= 2]


def row_sources(z, core):
    down = z >= 1
    up = z == SIDE - 1
    first = core == 0
    return [jnp.where(first, down, up), jnp.where(first, up, down), core == 1]


KINDS = {
    "q0": ("ahead", 0, 0),
    "qa": ("ahead", 1, 3),
    "qb": ("ahead", 3, 1),
    "q2": ("ahead", 2, 2),
    "rc": ("two", 0, 0),
    "sa": ("row", 1, 3),
    "sb": ("row", 3, 1),
    "x2": ("row", 2, 2),
}
PATHS = {
    "q0": lambda x, z, c: (x + 1, z, c),
    "w": lambda x, z, c: (x - 1, z, c) if z >= 2 else None,
    "rc": lambda x, z, c: (x - 1, z, c) if z >= 2 else (x + 1, z, c),
    "qa": lambda x, z, c: (x, z + side(c, False), c),
    "qb": lambda x, z, c: (x, z + side(c, True), c),
    "q2": lambda x, z, c: (x, z + side(c, False), c),
    "sa": lambda x, z, c: (x, z + side(c, False), c),
    "sb": lambda x, z, c: (x, z + side(c, True), c),
    "x2": lambda x, z, c: (x - 1, z, c) if z <= 1 else (x + 1, z, c),
}


def other_core(x, z, c):
    return x, z, 1 - c


def shards(voltages, pair_table, bad_feeds):
    here = lax.axis_index("blk").astype(jnp.int32)
    freq = lax.axis_index("freq").astype(jnp.int32)
    freq_count = lax.axis_size("freq")
    _, channels, parts, rows, samples = voltages.shape
    group = channels // freq_count
    width = rows * freq_count

    inputs = here * width + jnp.arange(width, dtype=jnp.int32)
    flagged = jnp.any((inputs // 2)[:, None] == bad_feeds[None, :], axis=-1)
    keep = jnp.where(flagged, 0.0, 1.0).astype(jnp.float32)[:, None]
    keep = jnp.broadcast_to(keep, (width, samples))
    info = jnp.concatenate([here[None], pair_table[:, 0]])
    shape = (pair_table.shape[0], group, parts, width, width)
    firsts = [sum(CHUNKS[:number]) for number in range(len(CHUNKS))]
    done = {}
    picked = {}

    def corner_turn(number, earlier):
        count = CHUNKS[number]

        def piece(shift):
            start = ((freq + shift) % freq_count) * group + firsts[number]
            return lax.dynamic_slice_in_dim(voltages[0], start, count, 0)

        pieces = [piece(0)]
        for shift in (1, 2, 3):
            pairs = [(source, (source + shift) % freq_count) for source in range(freq_count)]
            pieces.append(lax.ppermute(after(piece(shift), *earlier), "freq", pairs))
        return gather_rows(freq[None], pieces, keep)

    def pick(number):
        if number not in picked:
            picked[number] = choose(
                row_sources, 3, info, done["own", number], done["rc", number], f"pick3_{number}"
            )
        return picked[number]

    def tiles(visibility, index, number, items):
        slots, fars = [], []
        for name in items:
            if name == "own":
                slots.append(("own", 0, 0, False))
                continue
            slots.append((*KINDS[name], False))
            fars.append(done[name, number])
            slots.append(("mixed", 0, 0, False) if name == "rc" else (*KINDS[name], True))
            fars.append(done[name + "x", number])
        slots.sort(key=lambda slot: slot[0] == "own")
        return correlate(
            visibility, shape, info, done["own", number], fars, slots, firsts[number], f"tiles_k{index}"
        )

    def step(name, number):
        earlier = [done[other] for other in LATER.get((name, number), ())]
        if name == "own":
            return corner_turn(number, earlier)
        if name == "rc":
            value = choose(far_column, 1, info, done["w", number], done["q0", number], f"pick_{number}")[0]
        elif name in ("sa", "sb", "rcx"):
            value = pick(number)[("sa", "sb", "rcx").index(name)]
        elif name.endswith("x") and name != "x2":
            value = done[name[:-1], number]
        else:
            value = done[{"q0": "own", "w": "own", "qa": "q0", "qb": "q0", "q2": "qa", "x2": "q2"}[name], number]
        return fetch(after(value, *earlier), PATHS.get(name, other_core))

    visibility = None
    for name, number in ORDER:
        with jax.named_scope(f"n_{name}_{number}"):
            if name == "tiles":
                visibility = tiles(visibility, number, *KERNELS[number])
                done[name, number] = visibility
            else:
                done[name, number] = step(name, number)
    return visibility


def solution(mesh):
    placed = (P("blk", None, None, "freq", None), P("blk", None), P())
    return jax.shard_map(
        shards,
        mesh=mesh,
        in_specs=placed,
        out_specs=P("blk", "freq", None, None, None),
        check_vma=False,
    )
```
